32 devices in a mesh: seq: 8 (over y, x, core), head: 4 (over z).
Axes of the slice: x: 2, y: 2, z: 4, core: 2. Of those that a mesh axis runs over, the one named last changes fastest.
Arguments:
- queries: bfloat16 [1024, 32, 576], P('seq', 'head'), may hold values from -64 to 64
- latent: bfloat16 [1024, 576], P('seq'), may hold values from -8 to 8
- grad_out: bfloat16 [1024, 32, 512], P('seq', 'head'), may hold values from -6 to 6
- lookback: int32 [1024], P('seq'), may hold values from 0 to 256
Outputs:
- grad_queries: bfloat16 [1024, 32, 576], P('seq', 'head')
- grad_latent: bfloat16 [1024, 576], P('seq')
The draws below stay inside these ranges and needn't reach their ends.
All inputs are finite; a program needn't handle non-finite values.
Results may differ from the reference program's by a relative error of at most 0.0049.
Values may be sent and summed in bfloat16 or wider, within the bound.
A program may use at most 64 MiB of HBM per device.

```python
import jax
import jax.numpy as jnp
from jax import lax

LATENT = 512
ROPE = 64
NOPE = 128
TOK_DEV = 128
KEY_DIM = 576
HEADS = 32
TOKENS = 1024
N_SEQ = 8


def paired_draw(key):
    base = jax.random.fold_in(key, 11)
    latent_key, query_key = jax.random.split(base, 2)
    latent = jnp.clip(jax.random.normal(latent_key, (TOKENS, KEY_DIM), jnp.float32), -6.0, 6.0)
    queries = jnp.clip(jax.random.normal(query_key, (TOKENS, HEADS, KEY_DIM), jnp.float32), -6.0, 6.0)
    return (latent, queries)


def draw_queries(key, part):
    return paired_draw(key)[1].astype(jnp.bfloat16)


def draw_latent(key, part):
    return paired_draw(key)[0].astype(jnp.bfloat16)


def touch_ends(array, key, least, largest):
    spot = [jax.random.randint(jax.random.fold_in(key, axis), (), 0, length) for axis, length in enumerate(array.shape)]
    main_axis = array.shape.index(max(array.shape))
    next_to = spot[:main_axis] + [(spot[main_axis] + 1) % array.shape[main_axis]] + spot[main_axis + 1:]
    return array.at[tuple(spot)].set(least).at[tuple(next_to)].set(largest)


def steps_of(key, dims, shards, smallest, high):
    loudness, own = 1.0, jax.random.fold_in(key, 6)
    for position, parts in shards:
        heights = jnp.exp(jax.random.uniform(jax.random.fold_in(own, position), (parts,), jnp.float32, smallest / len(shards), high / len(shards)))
        loudness = loudness * jnp.repeat(heights, dims[position] // parts).reshape([-1 if axis == position else 1 for axis in range(len(dims))])
    return loudness


def gaussian(own_key, extent, width, limit, cuts=(), kind=jnp.bfloat16):
    entries = width * jax.random.normal(own_key, extent, jnp.float32)
    if cuts:
        entries = entries * steps_of(own_key, extent, cuts, -0.22, 0.18)
    return jnp.clip(entries, -limit, limit).astype(kind)


def setup_inputs(seed: int = 0) -> dict:
    keys = jax.random.split(jax.random.key(seed), 5)
    queries = draw_queries(jax.random.fold_in(keys[4], 71), 0)
    latent = draw_latent(jax.random.fold_in(keys[4], 71), 0)
    grad_out = gaussian(keys[2], (TOKENS, HEADS, LATENT), 1.0, 6.0, ((0, 8), (1, 4)))
    lookback = touch_ends(jax.random.randint(keys[3], (TOKENS,), 0, 2 * TOK_DEV + 1), jax.random.fold_in(keys[3], 1), 0, 2 * TOK_DEV).astype(jnp.int32)
    return {"queries": queries, "latent": latent, "grad_out": grad_out, "lookback": lookback}


def reference(queries, latent, grad_out, lookback):
    score_scale = (NOPE + ROPE) ** -0.5
    padding = jnp.zeros((2 * TOK_DEV, KEY_DIM), jnp.bfloat16)
    key_source = jnp.concatenate([padding, latent], axis=0)
    initial = jnp.zeros((TOKENS + 2 * TOK_DEV, KEY_DIM), jnp.float32)

    def advance(carried, block_id):
        first_row = (block_id * TOK_DEV).astype(jnp.int32)
        query_rows = lax.dynamic_slice_in_dim(queries, first_row, TOK_DEV, 0).reshape(TOK_DEV * HEADS, KEY_DIM)
        grad_rows = lax.dynamic_slice_in_dim(grad_out, first_row, TOK_DEV, 0).reshape(TOK_DEV * HEADS, LATENT)
        reach = lax.dynamic_slice_in_dim(lookback, first_row, TOK_DEV, 0)
        key_rows = lax.dynamic_slice_in_dim(key_source, first_row, 3 * TOK_DEV, 0)
        query_pos = first_row + jnp.arange(TOK_DEV, dtype=jnp.int32)
        key_pos = first_row - 2 * TOK_DEV + jnp.arange(3 * TOK_DEV, dtype=jnp.int32)
        allowed = (key_pos[None, :] >= 0) & (key_pos[None, :] <= query_pos[:, None]) & (key_pos[None, :] >= query_pos[:, None] - reach[:, None])
        allowed = jnp.broadcast_to(allowed[:, None, :], (TOK_DEV, HEADS, 3 * TOK_DEV)).reshape(TOK_DEV * HEADS, 3 * TOK_DEV)
        scores = jnp.dot(query_rows, key_rows.T, preferred_element_type=jnp.float32) * score_scale
        masked = jnp.where(allowed, scores, -jnp.inf)
        highest = jnp.max(masked, axis=-1, keepdims=True)
        weights = jnp.exp(masked - highest)
        weights = weights / jnp.sum(weights, axis=-1, keepdims=True)
        grad_weights = jnp.dot(grad_rows, key_rows[:, :LATENT].T, preferred_element_type=jnp.float32)
        row_dot = jnp.sum(weights * grad_weights, axis=-1, keepdims=True)
        grad_scores = (weights * (grad_weights - row_dot) * score_scale).astype(jnp.bfloat16)
        weights_half = weights.astype(jnp.bfloat16)
        grad_query = jnp.dot(grad_scores, key_rows, preferred_element_type=jnp.float32).astype(jnp.bfloat16)
        grad_keys = jnp.dot(grad_scores.T, query_rows, preferred_element_type=jnp.float32)
        grad_values = jnp.dot(weights_half.T, grad_rows, preferred_element_type=jnp.float32)
        combined = grad_keys + jnp.pad(grad_values, ((0, 0), (0, ROPE)))
        window = lax.dynamic_slice_in_dim(carried, first_row, 3 * TOK_DEV, 0)
        carried = lax.dynamic_update_slice_in_dim(carried, window + combined, first_row, 0)
        return carried, grad_query

    carried, grad_blocks = lax.scan(advance, initial, jnp.arange(N_SEQ, dtype=jnp.int32))
    grad_queries = grad_blocks.reshape(TOKENS, HEADS, KEY_DIM)
    grad_latent = carried[2 * TOK_DEV:].astype(jnp.bfloat16)
    return grad_queries, grad_latent
```

```python
import functools

import jax
import jax.numpy as jnp
from jax import lax
from jax.experimental import pallas as pl
from jax.experimental.pallas import tpu as pltpu
from jax.sharding import PartitionSpec as P

ROPE = 64
NOPE = 128
MESH = pl.DeviceIdType.MESH
F32 = jnp.float32
BF16 = jnp.bfloat16


def dot(a, b, trans_b=False):
    dims = (((1,), (1 if trans_b else 0,)), ((), ()))
    return lax.dot_general(a, b, dims, preferred_element_type=F32)


def kernel(
    n_seq, n_head, rows,
    q_hbm, k_hbm, g_hbm, look_ref, gq_hbm, gl_ref,
    q_v, g_v, g_wide, g_t, keys_t, keys, scores, grad_w, d_scores, weights, gq_v,
    part_out, part_in, own_sum, head_out, head_in, final,
    load_sem, gq_sem, key_send, key_recv, part_send, part_recv,
    head_send, head_recv, final_send, final_recv,
):
    heads, key_width, tok = q_hbm.shape
    value_width = g_hbm.shape[1]
    cols = heads * tok
    scale = (NOPE + ROPE) ** (-0.5)
    seq, head = lax.axis_index("seq"), lax.axis_index("head")
    ahead = [lax.rem(seq + d, n_seq) for d in (1, 2)]
    behind = [lax.rem(seq + n_seq - d, n_seq) for d in (1, 2)]
    peers = [lax.rem(head + 1 + i, n_head) for i in range(n_head - 1)]

    own_copy = pltpu.make_async_copy(k_hbm, keys_t.at[2], load_sem.at[0])
    own_copy.start()
    g_copy = pltpu.make_async_copy(g_hbm, g_v, load_sem.at[1])
    g_copy.start()
    q_copies = [
        pltpu.make_async_copy(q_hbm.at[h], q_v.at[:, h * tok:(h + 1) * tok], load_sem.at[2 + h])
        for h in range(heads)
    ]
    for copy in q_copies:
        copy.start()

    barrier = pltpu.get_barrier_semaphore()
    for other in ahead + behind:
        pl.semaphore_signal(barrier, inc=1, device_id=(other, head), device_id_type=MESH)
    for other in peers:
        pl.semaphore_signal(barrier, inc=1, device_id=(seq, other), device_id_type=MESH)
    pl.semaphore_wait(barrier, 4 + n_head - 1)

    own_copy.wait()
    key_copies = [
        pltpu.make_async_remote_copy(
            src_ref=keys_t.at[2], dst_ref=keys_t.at[1 - d],
            send_sem=key_send.at[d], recv_sem=key_recv.at[d],
            device_id=(ahead[d], head), device_id_type=MESH,
        )
        for d in range(2)
    ]
    for copy in key_copies:
        copy.start()

    keys[2 * tok:, :] = keys_t[2].T
    g_copy.wait()
    for c in range(value_width // 128):
        part = slice(c * 128, (c + 1) * 128)
        g_wide[c] = g_v[:, part].astype(F32)
        for h in range(heads):
            block = g_wide[c, pl.ds(h, tok, stride=heads), :].astype(BF16)
            g_t[part, h * tok:(h + 1) * tok] = block.T
    for copy in q_copies:
        copy.wait()
    own_keys = keys[2 * tok:, :]
    scores[2 * tok:, :] = dot(own_keys, q_v[...])
    grad_w[2 * tok:, :] = dot(own_keys[:, :value_width], g_t[...])

    for copy in key_copies:
        copy.wait_recv()
    for d in range(2):
        keys[d * tok:(d + 1) * tok, :] = keys_t[d].T
    far_keys = keys[:2 * tok, :]
    scores[:2 * tok, :] = dot(far_keys, q_v[...])
    grad_w[:2 * tok, :] = dot(far_keys[:, :value_width], g_t[...])

    key_pos = lax.broadcasted_iota(jnp.int32, (3 * tok, tok), 0)
    query_pos = lax.broadcasted_iota(jnp.int32, (3 * tok, tok), 1) + 2 * tok
    allowed = (
        (key_pos <= query_pos)
        & (key_pos >= query_pos - look_ref[...])
        & (key_pos >= (2 - seq) * tok)
    )
    for h in range(heads):
        span = slice(h * tok, (h + 1) * tok)
        masked = jnp.where(allowed, scores[:, span] * scale, -jnp.inf)
        weight = jnp.exp(masked - jnp.max(masked, axis=0, keepdims=True))
        weight = weight * (1.0 / jnp.sum(weight, axis=0, keepdims=True))
        grad_weight = grad_w[:, span]
        row_dot = jnp.sum(weight * grad_weight, axis=0, keepdims=True)
        d_scores[:, span] = (weight * (grad_weight - row_dot) * scale).astype(BF16)
        weights[:, span] = weight.astype(BF16)

    def partial_sum(first, last):
        q_part = dot(q_v[...], d_scores[first:last, :], True)
        g_part = dot(g_t[...], weights[first:last, :], True)
        return q_part[:value_width] + g_part, q_part[value_width:]

    top, bottom = partial_sum(0, 2 * tok)
    for d in range(2):
        part_out[d, :value_width, :] = top[:, d * tok:(d + 1) * tok].astype(BF16)
        part_out[d, value_width:key_width, :] = bottom[:, d * tok:(d + 1) * tok].astype(BF16)

    def piece(i):
        return pl.ds(pl.multiple_of(lax.rem(head + 1 + i, n_head) * rows, 16), rows)

    part_copies = []
    for i in range(n_head):
        for d in range(2):
            copy = pltpu.make_async_remote_copy(
                src_ref=part_out.at[d, piece(i)], dst_ref=part_in.at[d, piece(i)],
                send_sem=part_send.at[d, i], recv_sem=part_recv.at[d, i],
                device_id=(behind[1 - d], head), device_id_type=MESH,
            )
            copy.start()
            part_copies.append(copy)

    top, bottom = partial_sum(2 * tok, 3 * tok)
    own_sum[:value_width, :] = top
    own_sum[value_width:key_width, :] = bottom

    def reduce_piece(i):
        for copy in part_copies[2 * i:2 * i + 2]:
            copy.wait_recv()
        here = piece(i)
        return own_sum[here, :] + part_in[0, here, :].astype(F32) + part_in[1, here, :].astype(F32)

    gq_copies = []

    def grad_queries(first, last):
        all_keys = jnp.concatenate([keys_t[0], keys_t[1], keys_t[2]], axis=1)
        span = slice(first * tok, last * tok)
        gq_v[:, span] = dot(all_keys, d_scores[:, span]).astype(BF16)
        for h in range(first, last):
            copy = pltpu.make_async_copy(
                gq_v.at[:, h * tok:(h + 1) * tok], gq_hbm.at[h], gq_sem.at[h]
            )
            copy.start()
            gq_copies.append(copy)

    grad_queries(0, heads)

    head_copies = []
    for i in range(n_head - 1):
        head_out[i] = reduce_piece(i).astype(BF16)
        copy = pltpu.make_async_remote_copy(
            src_ref=head_out.at[i], dst_ref=head_in.at[i],
            send_sem=head_send.at[i], recv_sem=head_recv.at[i],
            device_id=(seq, peers[i]), device_id_type=MESH,
        )
        copy.start()
        head_copies.append(copy)
    total = reduce_piece(n_head - 1)
    for i in range(n_head - 1):
        head_copies[i].wait_recv()
        total = total + head_in[i].astype(F32)
    mine = piece(n_head - 1)
    final[mine, :] = total.astype(BF16)
    final_copies = []
    for i in range(n_head - 1):
        copy = pltpu.make_async_remote_copy(
            src_ref=final.at[mine], dst_ref=final.at[mine],
            send_sem=final_send.at[i], recv_sem=final_recv.at[i],
            device_id=(seq, peers[i]), device_id_type=MESH,
        )
        copy.start()
        final_copies.append(copy)
    for copy in final_copies:
        copy.wait_recv()
    gl_ref[...] = final[:key_width, :]
    for copy in key_copies + part_copies + head_copies + final_copies:
        copy.wait_send()
    for copy in gq_copies:
        copy.wait()


def on_device(n_seq, n_head, queries, latent, grad_out, lookback):
    tok, heads, key_width = queries.shape
    value_width = grad_out.shape[2]
    cols = heads * tok
    rows = -(-key_width // (n_head * 16)) * 16
    padded = rows * n_head
    dma = pltpu.SemaphoreType.DMA
    flops = 2 * 3 * tok * cols * (3 * key_width + 2 * value_width)
    grad_q, grad_l = pl.pallas_call(
        functools.partial(kernel, n_seq, n_head, rows),
        out_shape=(
            jax.ShapeDtypeStruct((heads, key_width, tok), BF16),
            jax.ShapeDtypeStruct((key_width, tok), BF16),
        ),
        in_specs=[pl.BlockSpec(memory_space=pl.ANY)] * 3
        + [pl.BlockSpec(memory_space=pltpu.VMEM)],
        out_specs=(pl.BlockSpec(memory_space=pl.ANY), pl.BlockSpec(memory_space=pltpu.VMEM)),
        scratch_shapes=[
            pltpu.VMEM((key_width, cols), BF16),
            pltpu.VMEM((cols, value_width), BF16),
            pltpu.VMEM((value_width // 128, cols, 128), F32),
            pltpu.VMEM((value_width, cols), BF16),
            pltpu.VMEM((3, key_width, tok), BF16),
            pltpu.VMEM((3 * tok, key_width), BF16),
            pltpu.VMEM((3 * tok, cols), F32),
            pltpu.VMEM((3 * tok, cols), F32),
            pltpu.VMEM((3 * tok, cols), BF16),
            pltpu.VMEM((3 * tok, cols), BF16),
            pltpu.VMEM((key_width, cols), BF16),
            pltpu.VMEM((2, padded, tok), BF16),
            pltpu.VMEM((2, padded, tok), BF16),
            pltpu.VMEM((padded, tok), F32),
            pltpu.VMEM((n_head - 1, rows, tok), BF16),
            pltpu.VMEM((n_head - 1, rows, tok), BF16),
            pltpu.VMEM((padded, tok), BF16),
            dma((2 + heads,)),
            dma((heads,)),
            dma((2,)),
            dma((2,)),
            dma((2, n_head)),
            dma((2, n_head)),
            dma((n_head - 1,)),
            dma((n_head - 1,)),
            dma((n_head - 1,)),
            dma((n_head - 1,)),
        ],
        compiler_params=pltpu.CompilerParams(
            collective_id=0, has_side_effects=True, vmem_limit_bytes=40 * 1024 * 1024
        ),
        cost_estimate=pl.CostEstimate(
            flops=flops, bytes_accessed=8 * cols * key_width, transcendentals=3 * tok * cols
        ),
        name="latent_backward",
    )(
        queries.transpose(1, 2, 0),
        latent.T,
        grad_out.reshape(tok * heads, value_width),
        lookback.reshape(1, tok),
    )
    return grad_q.transpose(2, 0, 1), grad_l.T


def solution(mesh):
    return jax.shard_map(
        functools.partial(on_device, mesh.shape["seq"], mesh.shape["head"]),
        mesh=mesh,
        in_specs=(P("seq", "head", None), P("seq", None), P("seq", "head", None), P("seq")),
        out_specs=(P("seq", "head", None), P("seq", None)),
        check_vma=False,
    )
```

```python
import functools

import jax
import jax.numpy as jnp
from jax import lax
from jax.experimental import pallas as pl
from jax.experimental.pallas import tpu as pltpu
from jax.sharding import PartitionSpec as P

ROPE = 64
NOPE = 128
MESH = pl.DeviceIdType.MESH
F32 = jnp.float32
BF16 = jnp.bfloat16


def dot(a, b, trans_b=False):
    dims = (((1,), (1 if trans_b else 0,)), ((), ()))
    return lax.dot_general(a, b, dims, preferred_element_type=F32)


def kernel(
    n_seq, n_head, rows,
    q_hbm, k_hbm, g_hbm, look_hbm, gq_hbm, gl_ref,
    look_ref, q_v, g_v, g_wide, g_t, keys_t, keys, scores, grad_w, d_scores, weights, gq_v,
    part_out, part_in, own_sum, head_out, head_in, final,
    load_sem, gq_sem, key_send, key_recv, part_send, part_recv,
    head_send, head_recv, final_send, final_recv,
):
    heads, key_width, tok = q_hbm.shape
    value_width = g_hbm.shape[1]
    cols = heads * tok
    scale = (NOPE + ROPE) ** (-0.5)
    seq, head = lax.axis_index("seq"), lax.axis_index("head")
    ahead = [lax.rem(seq + d, n_seq) for d in (1, 2)]
    behind = [lax.rem(seq + n_seq - d, n_seq) for d in (1, 2)]
    peers = [lax.rem(head + 1 + i, n_head) for i in range(n_head - 1)]

    own_copy = pltpu.make_async_copy(k_hbm, keys_t.at[2], load_sem.at[0])
    own_copy.start()
    g_copy = pltpu.make_async_copy(g_hbm, g_v, load_sem.at[1])
    g_copy.start()
    q_copies = [
        pltpu.make_async_copy(q_hbm.at[h], q_v.at[:, h * tok:(h + 1) * tok], load_sem.at[2 + h])
        for h in range(heads)
    ]
    look_copy = pltpu.make_async_copy(look_hbm, look_ref, load_sem.at[2 + heads])
    for copy in q_copies + [look_copy]:
        copy.start()

    barrier = pltpu.get_barrier_semaphore()
    for other in ahead + behind:
        pl.semaphore_signal(barrier, inc=1, device_id=(other, head), device_id_type=MESH)
    for other in peers:
        pl.semaphore_signal(barrier, inc=1, device_id=(seq, other), device_id_type=MESH)
    pl.semaphore_wait(barrier, 4 + n_head - 1)

    own_copy.wait()
    key_copies = [
        pltpu.make_async_remote_copy(
            src_ref=keys_t.at[2], dst_ref=keys_t.at[1 - d],
            send_sem=key_send.at[d], recv_sem=key_recv.at[d],
            device_id=(ahead[d], head), device_id_type=MESH,
        )
        for d in range(2)
    ]
    for copy in key_copies:
        copy.start()

    keys[2 * tok:, :] = keys_t[2].T
    g_copy.wait()
    for c in range(value_width // 128):
        part = slice(c * 128, (c + 1) * 128)
        g_wide[c] = g_v[:, part].astype(F32)
        for h in range(heads):
            block = g_wide[c, pl.ds(h, tok, stride=heads), :].astype(BF16)
            g_t[part, h * tok:(h + 1) * tok] = block.T
    for copy in q_copies:
        copy.wait()
    own_keys = keys[2 * tok:, :]
    scores[2 * tok:, :] = dot(own_keys, q_v[...])
    grad_w[2 * tok:, :] = dot(own_keys[:, :value_width], g_t[...])

    for copy in key_copies:
        copy.wait_recv()
    for d in range(2):
        keys[d * tok:(d + 1) * tok, :] = keys_t[d].T
    far_keys = keys[:2 * tok, :]
    scores[:2 * tok, :] = dot(far_keys, q_v[...])
    grad_w[:2 * tok, :] = dot(far_keys[:, :value_width], g_t[...])

    look_copy.wait()
    key_pos = lax.broadcasted_iota(jnp.int32, (3 * tok, tok), 0)
    query_pos = lax.broadcasted_iota(jnp.int32, (3 * tok, tok), 1) + 2 * tok
    allowed = (
        (key_pos <= query_pos)
        & (key_pos >= query_pos - look_ref[...])
        & (key_pos >= (2 - seq) * tok)
    )
    for h in range(heads):
        span = slice(h * tok, (h + 1) * tok)
        masked = jnp.where(allowed, scores[:, span] * scale, -jnp.inf)
        weight = jnp.exp(masked - jnp.max(masked, axis=0, keepdims=True))
        weight = weight * (1.0 / jnp.sum(weight, axis=0, keepdims=True))
        grad_weight = grad_w[:, span]
        row_dot = jnp.sum(weight * grad_weight, axis=0, keepdims=True)
        d_scores[:, span] = (weight * (grad_weight - row_dot) * scale).astype(BF16)
        weights[:, span] = weight.astype(BF16)

    def partial_sum(first, last):
        q_part = dot(q_v[...], d_scores[first:last, :], True)
        g_part = dot(g_t[...], weights[first:last, :], True)
        return q_part[:value_width] + g_part, q_part[value_width:]

    top, bottom = partial_sum(0, 2 * tok)
    for d in range(2):
        part_out[d, :value_width, :] = top[:, d * tok:(d + 1) * tok].astype(BF16)
        part_out[d, value_width:key_width, :] = bottom[:, d * tok:(d + 1) * tok].astype(BF16)

    def piece(i):
        return pl.ds(pl.multiple_of(lax.rem(head + 1 + i, n_head) * rows, 16), rows)

    part_copies = []
    for i in range(n_head):
        for d in range(2):
            copy = pltpu.make_async_remote_copy(
                src_ref=part_out.at[d, piece(i)], dst_ref=part_in.at[d, piece(i)],
                send_sem=part_send.at[d, i], recv_sem=part_recv.at[d, i],
                device_id=(behind[1 - d], head), device_id_type=MESH,
            )
            copy.start()
            part_copies.append(copy)

    top, bottom = partial_sum(2 * tok, 3 * tok)
    own_sum[:value_width, :] = top
    own_sum[value_width:key_width, :] = bottom

    def reduce_piece(i):
        for copy in part_copies[2 * i:2 * i + 2]:
            copy.wait_recv()
        here = piece(i)
        return own_sum[here, :] + part_in[0, here, :].astype(F32) + part_in[1, here, :].astype(F32)

    gq_copies = []

    def grad_queries(first, last):
        all_keys = jnp.concatenate([keys_t[0], keys_t[1], keys_t[2]], axis=1)
        span = slice(first * tok, last * tok)
        gq_v[:, span] = dot(all_keys, d_scores[:, span]).astype(BF16)
        for h in range(first, last):
            copy = pltpu.make_async_copy(
                gq_v.at[:, h * tok:(h + 1) * tok], gq_hbm.at[h], gq_sem.at[h]
            )
            copy.start()
            gq_copies.append(copy)

    grad_queries(0, heads)

    head_copies = []
    for i in range(n_head - 1):
        head_out[i] = reduce_piece(i).astype(BF16)
        copy = pltpu.make_async_remote_copy(
            src_ref=head_out.at[i], dst_ref=head_in.at[i],
            send_sem=head_send.at[i], recv_sem=head_recv.at[i],
            device_id=(seq, peers[i]), device_id_type=MESH,
        )
        copy.start()
        head_copies.append(copy)
    total = reduce_piece(n_head - 1)
    for i in range(n_head - 1):
        head_copies[i].wait_recv()
        total = total + head_in[i].astype(F32)
    mine = piece(n_head - 1)
    final[mine, :] = total.astype(BF16)
    final_copies = []
    for i in range(n_head - 1):
        copy = pltpu.make_async_remote_copy(
            src_ref=final.at[mine], dst_ref=final.at[mine],
            send_sem=final_send.at[i], recv_sem=final_recv.at[i],
            device_id=(seq, peers[i]), device_id_type=MESH,
        )
        copy.start()
        final_copies.append(copy)
    for copy in final_copies:
        copy.wait_recv()
    gl_ref[...] = final[:key_width, :]
    for copy in key_copies + part_copies + head_copies + final_copies:
        copy.wait_send()
    for copy in gq_copies:
        copy.wait()


def write_back(gq_ref, gl_ref, gq_out, gl_out, sem):
    heads = gq_ref.shape[0]
    copies = [pltpu.make_async_copy(gl_ref, gl_out, sem.at[heads])]
    for h in range(heads):
        copies.append(pltpu.make_async_copy(gq_ref.at[h], gq_out.at[h], sem.at[h]))
    for copy in copies:
        copy.start()
    for copy in copies:
        copy.wait()


def on_device(n_seq, n_head, queries, latent, grad_out, lookback):
    tok, heads, key_width = queries.shape
    value_width = grad_out.shape[2]
    cols = heads * tok
    rows = -(-key_width // (n_head * 16)) * 16
    padded = rows * n_head
    dma = pltpu.SemaphoreType.DMA
    flops = 2 * 3 * tok * cols * (3 * key_width + 2 * value_width)
    operands = [
        pltpu.with_memory_space_constraint(value, pltpu.HBM)
        for value in (
            queries.transpose(1, 2, 0),
            latent.T,
            grad_out.reshape(tok * heads, value_width),
            lookback.reshape(1, tok),
        )
    ]
    grad_q, grad_l = pl.pallas_call(
        functools.partial(kernel, n_seq, n_head, rows),
        out_shape=(
            jax.ShapeDtypeStruct((heads, key_width, tok), BF16),
            jax.ShapeDtypeStruct((key_width, tok), BF16),
        ),
        in_specs=[pl.BlockSpec(memory_space=pltpu.HBM)] * 4,
        out_specs=(pl.BlockSpec(memory_space=pl.ANY), pl.BlockSpec(memory_space=pltpu.VMEM)),
        scratch_shapes=[
            pltpu.VMEM((1, tok), jnp.int32),
            pltpu.VMEM((key_width, cols), BF16),
            pltpu.VMEM((cols, value_width), BF16),
            pltpu.VMEM((value_width // 128, cols, 128), F32),
            pltpu.VMEM((value_width, cols), BF16),
            pltpu.VMEM((3, key_width, tok), BF16),
            pltpu.VMEM((3 * tok, key_width), BF16),
            pltpu.VMEM((3 * tok, cols), F32),
            pltpu.VMEM((3 * tok, cols), F32),
            pltpu.VMEM((3 * tok, cols), BF16),
            pltpu.VMEM((3 * tok, cols), BF16),
            pltpu.VMEM((key_width, cols), BF16),
            pltpu.VMEM((2, padded, tok), BF16),
            pltpu.VMEM((2, padded, tok), BF16),
            pltpu.VMEM((padded, tok), F32),
            pltpu.VMEM((n_head - 1, rows, tok), BF16),
            pltpu.VMEM((n_head - 1, rows, tok), BF16),
            pltpu.VMEM((padded, tok), BF16),
            dma((3 + heads,)),
            dma((heads,)),
            dma((2,)),
            dma((2,)),
            dma((2, n_head)),
            dma((2, n_head)),
            dma((n_head - 1,)),
            dma((n_head - 1,)),
            dma((n_head - 1,)),
            dma((n_head - 1,)),
        ],
        compiler_params=pltpu.CompilerParams(
            collective_id=0, has_side_effects=True, vmem_limit_bytes=40 * 1024 * 1024
        ),
        cost_estimate=pl.CostEstimate(
            flops=flops, bytes_accessed=8 * cols * key_width, transcendentals=3 * tok * cols
        ),
        name="latent_backward",
    )(*operands)
    grad_q, grad_l = pl.pallas_call(
        write_back,
        out_shape=(
            jax.ShapeDtypeStruct(grad_q.shape, BF16),
            jax.ShapeDtypeStruct(grad_l.shape, BF16),
        ),
        in_specs=[pl.BlockSpec(memory_space=pl.ANY)] * 2,
        out_specs=(pl.BlockSpec(memory_space=pltpu.HBM),) * 2,
        scratch_shapes=[dma((heads + 1,))],
        name="write_back",
    )(grad_q, grad_l)
    return grad_q.transpose(2, 0, 1), grad_l.T


def solution(mesh):
    return jax.shard_map(
        functools.partial(on_device, mesh.shape["seq"], mesh.shape["head"]),
        mesh=mesh,
        in_specs=(P("seq", "head", None), P("seq", None), P("seq", "head", None), P("seq")),
        out_specs=(P("seq", "head", None), P("seq", None)),
        check_vma=False,
    )
```

```python
import functools

import jax
import jax.numpy as jnp
from jax import lax
from jax.experimental import pallas as pl
from jax.experimental.pallas import tpu as pltpu
from jax.sharding import PartitionSpec as P

ROPE = 64
NOPE = 128
KEY_CHUNKS = 4
MESH = pl.DeviceIdType.MESH
F32 = jnp.float32
BF16 = jnp.bfloat16


def dot(a, b, trans_b=False):
    dims = (((1,), (1 if trans_b else 0,)), ((), ()))
    return lax.dot_general(a, b, dims, preferred_element_type=F32)


def kernel(
    n_seq, n_head, rows,
    q_hbm, k_hbm, g_hbm, look_hbm, gq_hbm, gl_ref,
    look_ref, q_v, g_v, g_wide, g_t, keys_t, keys, scores, grad_w, d_scores, weights, gq_v,
    part_out, part_in, relay_in, own_sum, head_out, head_in, final,
    load_sem, gq_sem, key_send, key_recv, part_send, part_recv, relay_recv,
    head_send, head_recv, final_send, final_recv,
):
    heads, key_width, tok = q_hbm.shape
    value_width = g_hbm.shape[1]
    cols = heads * tok
    scale = (NOPE + ROPE) ** (-0.5)
    seq, head = lax.axis_index("seq"), lax.axis_index("head")
    ahead = [lax.rem(seq + d, n_seq) for d in (1, 2)]
    behind = [lax.rem(seq + n_seq - d, n_seq) for d in (1, 2)]
    peers = [lax.rem(head + 1 + i, n_head) for i in range(n_head - 1)]

    own_copy = pltpu.make_async_copy(k_hbm, keys_t.at[2], load_sem.at[0])
    own_copy.start()
    g_copy = pltpu.make_async_copy(g_hbm, g_v, load_sem.at[1])
    g_copy.start()
    q_copies = [
        pltpu.make_async_copy(q_hbm.at[h], q_v.at[:, h * tok:(h + 1) * tok], load_sem.at[2 + h])
        for h in range(heads)
    ]
    look_copy = pltpu.make_async_copy(look_hbm, look_ref, load_sem.at[2 + heads])
    for copy in q_copies + [look_copy]:
        copy.start()

    barrier = pltpu.get_barrier_semaphore()
    for other in ahead + behind:
        pl.semaphore_signal(barrier, inc=1, device_id=(other, head), device_id_type=MESH)
    for other in peers:
        pl.semaphore_signal(barrier, inc=1, device_id=(seq, other), device_id_type=MESH)
    pl.semaphore_wait(barrier, 4 + n_head - 1)

    own_copy.wait()
    even = lax.rem(seq, 2) == 0
    chunk = key_width // KEY_CHUNKS

    def send_keys(source, target, c, other):
        span = pl.ds(c * chunk, chunk)
        return pltpu.make_async_remote_copy(
            src_ref=keys_t.at[source, span], dst_ref=keys_t.at[target, span],
            send_sem=key_send.at[source, target, c], recv_sem=key_recv.at[target, c],
            device_id=(other, head), device_id_type=MESH,
        )

    near_keys = [send_keys(2, 1, c, ahead[0]) for c in range(KEY_CHUNKS)]
    far_sends = [send_keys(2, 0, c, ahead[1]) for c in range(KEY_CHUNKS)]
    passed_on = [send_keys(1, 0, c, ahead[0]) for c in range(KEY_CHUNKS)]
    for copy in near_keys:
        copy.start()

    @pl.when(even)
    def _():
        for copy in far_sends:
            copy.start()

    keys[2 * tok:, :] = keys_t[2].T
    g_copy.wait()
    for c in range(value_width // 128):
        part = slice(c * 128, (c + 1) * 128)
        g_wide[c] = g_v[:, part].astype(F32)
        for h in range(heads):
            block = g_wide[c, pl.ds(h, tok, stride=heads), :].astype(BF16)
            g_t[part, h * tok:(h + 1) * tok] = block.T
    for copy in q_copies:
        copy.wait()
    own_keys = keys[2 * tok:, :]
    scores[2 * tok:, :] = dot(own_keys, q_v[...])
    grad_w[2 * tok:, :] = dot(own_keys[:, :value_width], g_t[...])

    @pl.when(even)
    def _():
        for c in range(KEY_CHUNKS):
            near_keys[c].wait_recv()
            passed_on[c].start()

    @pl.when(jnp.logical_not(even))
    def _():
        for copy in near_keys:
            copy.wait_recv()

    for copy in far_sends:
        copy.wait_recv()
    for d in range(2):
        keys[d * tok:(d + 1) * tok, :] = keys_t[d].T
    far_keys = keys[:2 * tok, :]
    scores[:2 * tok, :] = dot(far_keys, q_v[...])
    grad_w[:2 * tok, :] = dot(far_keys[:, :value_width], g_t[...])

    look_copy.wait()
    key_pos = lax.broadcasted_iota(jnp.int32, (3 * tok, tok), 0)
    query_pos = lax.broadcasted_iota(jnp.int32, (3 * tok, tok), 1) + 2 * tok
    allowed = (
        (key_pos <= query_pos)
        & (key_pos >= query_pos - look_ref[...])
        & (key_pos >= (2 - seq) * tok)
    )
    for h in range(heads):
        span = slice(h * tok, (h + 1) * tok)
        masked = jnp.where(allowed, scores[:, span] * scale, -jnp.inf)
        weight = jnp.exp(masked - jnp.max(masked, axis=0, keepdims=True))
        weight = weight * (1.0 / jnp.sum(weight, axis=0, keepdims=True))
        grad_weight = grad_w[:, span]
        row_dot = jnp.sum(weight * grad_weight, axis=0, keepdims=True)
        d_scores[:, span] = (weight * (grad_weight - row_dot) * scale).astype(BF16)
        weights[:, span] = weight.astype(BF16)

    def partial_sum(first, last):
        q_part = dot(q_v[...], d_scores[first:last, :], True)
        g_part = dot(g_t[...], weights[first:last, :], True)
        return q_part[:value_width] + g_part, q_part[value_width:]

    top, bottom = partial_sum(0, 2 * tok)
    for d in range(2):
        part_out[d, :value_width, :] = top[:, d * tok:(d + 1) * tok].astype(BF16)
        part_out[d, value_width:key_width, :] = bottom[:, d * tok:(d + 1) * tok].astype(BF16)

    def piece(i):
        return pl.ds(pl.multiple_of(lax.rem(head + 1 + i, n_head) * rows, 16), rows)

    def send_part(source, target_ref, recv_sem, i, other):
        return pltpu.make_async_remote_copy(
            src_ref=part_out.at[source, piece(i)], dst_ref=target_ref.at[piece(i)],
            send_sem=part_send.at[source, i], recv_sem=recv_sem.at[i],
            device_id=(other, head), device_id_type=MESH,
        )

    far_parts = [send_part(0, part_in.at[0], part_recv.at[0], i, behind[1]) for i in range(n_head)]
    near_parts = [send_part(1, part_in.at[1], part_recv.at[1], i, behind[0]) for i in range(n_head)]
    relayed = [send_part(0, relay_in, relay_recv, i, behind[0]) for i in range(n_head)]

    @pl.when(even)
    def _():
        for copy in far_parts:
            copy.start()
        for i in range(n_head):
            here = piece(i)
            relayed[i].wait_recv()
            joined = part_out[1, here, :].astype(F32) + relay_in[here, :].astype(F32)
            part_out[1, here, :] = joined.astype(BF16)
            near_parts[i].start()

    @pl.when(jnp.logical_not(even))
    def _():
        part_in[0] = jnp.zeros_like(part_in[0])
        for i in range(n_head):
            relayed[i].start()
        for copy in near_parts:
            copy.start()

    top, bottom = partial_sum(2 * tok, 3 * tok)
    own_sum[:value_width, :] = top
    own_sum[value_width:key_width, :] = bottom

    def reduce_piece(i):
        near_parts[i].wait_recv()

        @pl.when(even)
        def _():
            far_parts[i].wait_recv()

        here = piece(i)
        return own_sum[here, :] + part_in[0, here, :].astype(F32) + part_in[1, here, :].astype(F32)

    gq_copies = []

    def grad_queries(first, last):
        all_keys = jnp.concatenate([keys_t[0], keys_t[1], keys_t[2]], axis=1)
        span = slice(first * tok, last * tok)
        gq_v[:, span] = dot(all_keys, d_scores[:, span]).astype(BF16)
        for h in range(first, last):
            copy = pltpu.make_async_copy(
                gq_v.at[:, h * tok:(h + 1) * tok], gq_hbm.at[h], gq_sem.at[h]
            )
            copy.start()
            gq_copies.append(copy)

    grad_queries(0, heads)

    head_copies = []
    for i in range(n_head - 1):
        head_out[i] = reduce_piece(i).astype(BF16)
        copy = pltpu.make_async_remote_copy(
            src_ref=head_out.at[i], dst_ref=head_in.at[i],
            send_sem=head_send.at[i], recv_sem=head_recv.at[i],
            device_id=(seq, peers[i]), device_id_type=MESH,
        )
        copy.start()
        head_copies.append(copy)
    total = reduce_piece(n_head - 1)
    for i in range(n_head - 1):
        head_copies[i].wait_recv()
        total = total + head_in[i].astype(F32)
    mine = piece(n_head - 1)
    final[mine, :] = total.astype(BF16)
    final_copies = []
    for i in range(n_head - 1):
        copy = pltpu.make_async_remote_copy(
            src_ref=final.at[mine], dst_ref=final.at[mine],
            send_sem=final_send.at[i], recv_sem=final_recv.at[i],
            device_id=(seq, peers[i]), device_id_type=MESH,
        )
        copy.start()
        final_copies.append(copy)
    for copy in final_copies:
        copy.wait_recv()
    gl_ref[...] = final[:key_width, :]
    for copy in near_keys + near_parts + head_copies + final_copies:
        copy.wait_send()

    @pl.when(even)
    def _():
        for copy in far_sends + passed_on + far_parts:
            copy.wait_send()

    @pl.when(jnp.logical_not(even))
    def _():
        for copy in relayed:
            copy.wait_send()

    for copy in gq_copies:
        copy.wait()


def write_back(gq_ref, gl_ref, gq_out, gl_out, sem):
    heads = gq_ref.shape[0]
    copies = [pltpu.make_async_copy(gl_ref, gl_out, sem.at[heads])]
    for h in range(heads):
        copies.append(pltpu.make_async_copy(gq_ref.at[h], gq_out.at[h], sem.at[h]))
    for copy in copies:
        copy.start()
    for copy in copies:
        copy.wait()


def on_device(n_seq, n_head, queries, latent, grad_out, lookback):
    tok, heads, key_width = queries.shape
    value_width = grad_out.shape[2]
    cols = heads * tok
    rows = -(-key_width // (n_head * 16)) * 16
    padded = rows * n_head
    dma = pltpu.SemaphoreType.DMA
    flops = 2 * 3 * tok * cols * (3 * key_width + 2 * value_width)
    operands = [
        pltpu.with_memory_space_constraint(value, pltpu.HBM)
        for value in (
            queries.transpose(1, 2, 0),
            latent.T,
            grad_out.reshape(tok * heads, value_width),
            lookback.reshape(1, tok),
        )
    ]
    grad_q, grad_l = pl.pallas_call(
        functools.partial(kernel, n_seq, n_head, rows),
        out_shape=(
            jax.ShapeDtypeStruct((heads, key_width, tok), BF16),
            jax.ShapeDtypeStruct((key_width, tok), BF16),
        ),
        in_specs=[pl.BlockSpec(memory_space=pltpu.HBM)] * 4,
        out_specs=(pl.BlockSpec(memory_space=pl.ANY), pl.BlockSpec(memory_space=pltpu.VMEM)),
        scratch_shapes=[
            pltpu.VMEM((1, tok), jnp.int32),
            pltpu.VMEM((key_width, cols), BF16),
            pltpu.VMEM((cols, value_width), BF16),
            pltpu.VMEM((value_width // 128, cols, 128), F32),
            pltpu.VMEM((value_width, cols), BF16),
            pltpu.VMEM((3, key_width, tok), BF16),
            pltpu.VMEM((3 * tok, key_width), BF16),
            pltpu.VMEM((3 * tok, cols), F32),
            pltpu.VMEM((3 * tok, cols), F32),
            pltpu.VMEM((3 * tok, cols), BF16),
            pltpu.VMEM((3 * tok, cols), BF16),
            pltpu.VMEM((key_width, cols), BF16),
            pltpu.VMEM((2, padded, tok), BF16),
            pltpu.VMEM((2, padded, tok), BF16),
            pltpu.VMEM((padded, tok), BF16),
            pltpu.VMEM((padded, tok), F32),
            pltpu.VMEM((n_head - 1, rows, tok), BF16),
            pltpu.VMEM((n_head - 1, rows, tok), BF16),
            pltpu.VMEM((padded, tok), BF16),
            dma((3 + heads,)),
            dma((heads,)),
            dma((3, 2, KEY_CHUNKS)),
            dma((2, KEY_CHUNKS)),
            dma((2, n_head)),
            dma((2, n_head)),
            dma((n_head,)),
            dma((n_head - 1,)),
            dma((n_head - 1,)),
            dma((n_head - 1,)),
            dma((n_head - 1,)),
        ],
        compiler_params=pltpu.CompilerParams(
            collective_id=0, has_side_effects=True, vmem_limit_bytes=40 * 1024 * 1024
        ),
        cost_estimate=pl.CostEstimate(
            flops=flops, bytes_accessed=8 * cols * key_width, transcendentals=3 * tok * cols
        ),
        name="latent_backward",
    )(*operands)
    grad_q, grad_l = pl.pallas_call(
        write_back,
        out_shape=(
            jax.ShapeDtypeStruct(grad_q.shape, BF16),
            jax.ShapeDtypeStruct(grad_l.shape, BF16),
        ),
        in_specs=[pl.BlockSpec(memory_space=pltpu.VMEM)] * 2,
        out_specs=(pl.BlockSpec(memory_space=pltpu.HBM),) * 2,
        scratch_shapes=[dma((heads + 1,))],
        name="write_back",
    )(grad_q, grad_l)
    return grad_q.transpose(2, 0, 1), grad_l.T


def solution(mesh):
    return jax.shard_map(
        functools.partial(on_device, mesh.shape["seq"], mesh.shape["head"]),
        mesh=mesh,
        in_specs=(P("seq", "head", None), P("seq", None), P("seq", "head", None), P("seq")),
        out_specs=(P("seq", "head", None), P("seq", None)),
        check_vma=False,
    )
```

```python
import functools

import jax
import jax.numpy as jnp
from jax import lax
from jax.experimental import pallas as pl
from jax.experimental.pallas import tpu as pltpu
from jax.sharding import PartitionSpec as P

ROPE = 64
NOPE = 128
KEY_CHUNKS = 4
LOG2E = 1.4426950408889634
MESH = pl.DeviceIdType.MESH
F32 = jnp.float32
BF16 = jnp.bfloat16


def dot(a, b, trans_b=False):
    dims = (((1,), (1 if trans_b else 0,)), ((), ()))
    return lax.dot_general(a, b, dims, preferred_element_type=F32)


def kernel(
    n_seq, n_head, rows,
    q_hbm, k_hbm, g_hbm, look_hbm, gq_hbm, gl_ref,
    look_ref, q_v, g_v, g_wide, g_t, keys_t, keys, scores, grad_w, bias, part_sum, d_scores, weights, gq_v,
    part_out, part_in, relay_in, own_sum, head_out, head_in, final,
    load_sem, gq_sem, key_send, key_recv, part_send, part_recv, relay_recv,
    head_send, head_recv, final_send, final_recv,
):
    heads, key_width, tok = q_hbm.shape
    value_width = g_hbm.shape[1]
    cols = heads * tok
    scale = (NOPE + ROPE) ** (-0.5)
    scale2 = scale * LOG2E
    seq, head = lax.axis_index("seq"), lax.axis_index("head")
    ahead = [lax.rem(seq + d, n_seq) for d in (1, 2)]
    behind = [lax.rem(seq + n_seq - d, n_seq) for d in (1, 2)]
    peers = [lax.rem(head + 1 + i, n_head) for i in range(n_head - 1)]

    own_copy = pltpu.make_async_copy(k_hbm, keys_t.at[2], load_sem.at[0])
    own_copy.start()
    g_copy = pltpu.make_async_copy(g_hbm, g_v, load_sem.at[1])
    g_copy.start()
    q_copies = [
        pltpu.make_async_copy(q_hbm.at[h], q_v.at[:, h * tok:(h + 1) * tok], load_sem.at[2 + h])
        for h in range(heads)
    ]
    look_copy = pltpu.make_async_copy(look_hbm, look_ref, load_sem.at[2 + heads])
    for copy in q_copies + [look_copy]:
        copy.start()

    barrier = pltpu.get_barrier_semaphore()
    for other in ahead + behind:
        pl.semaphore_signal(barrier, inc=1, device_id=(other, head), device_id_type=MESH)
    for other in peers:
        pl.semaphore_signal(barrier, inc=1, device_id=(seq, other), device_id_type=MESH)
    pl.semaphore_wait(barrier, 4 + n_head - 1)

    own_copy.wait()
    even = lax.rem(seq, 2) == 0
    chunk = key_width // KEY_CHUNKS

    def send_keys(source, target, c, other):
        span = pl.ds(c * chunk, chunk)
        return pltpu.make_async_remote_copy(
            src_ref=keys_t.at[source, span], dst_ref=keys_t.at[target, span],
            send_sem=key_send.at[source, target, c], recv_sem=key_recv.at[target, c],
            device_id=(other, head), device_id_type=MESH,
        )

    near_keys = [send_keys(2, 1, c, ahead[0]) for c in range(KEY_CHUNKS)]
    far_sends = [send_keys(2, 0, c, ahead[1]) for c in range(KEY_CHUNKS)]
    passed_on = [send_keys(1, 0, c, ahead[0]) for c in range(KEY_CHUNKS)]
    for copy in near_keys:
        copy.start()

    @pl.when(even)
    def _():
        for copy in far_sends:
            copy.start()

    keys[2 * tok:, :] = keys_t[2].T
    g_copy.wait()
    for c in range(value_width // 128):
        part = slice(c * 128, (c + 1) * 128)
        g_wide[c] = g_v[:, part].astype(F32)
        for h in range(heads):
            block = g_wide[c, pl.ds(h, tok, stride=heads), :].astype(BF16)
            g_t[part, h * tok:(h + 1) * tok] = block.T
    for copy in q_copies:
        copy.wait()
    look_copy.wait()
    key_pos = lax.broadcasted_iota(jnp.int32, (3 * tok, tok), 0)
    query_pos = lax.broadcasted_iota(jnp.int32, (3 * tok, tok), 1) + 2 * tok
    allowed = (
        (key_pos <= query_pos)
        & (key_pos >= query_pos - look_ref[...])
        & (key_pos >= (2 - seq) * tok)
    )
    bias[...] = jnp.where(allowed, 0.0, -jnp.inf)
    own_keys = keys[2 * tok:, :]
    for h in range(0, heads, 2):
        span = slice(h * tok, (h + 2) * tok)
        own_bias = bias[2 * tok:, :]
        scores[2 * tok:, span] = dot(own_keys, q_v[:, span]) * scale2 + jnp.concatenate(
            [own_bias, own_bias], axis=1
        )
        grad_w[2 * tok:, span] = dot(own_keys[:, :value_width], g_t[:, span])

    @pl.when(even)
    def _():
        for c in range(KEY_CHUNKS):
            near_keys[c].wait_recv()
            passed_on[c].start()

    @pl.when(jnp.logical_not(even))
    def _():
        for copy in near_keys:
            copy.wait_recv()

    for copy in far_sends:
        copy.wait_recv()
    for d in range(2):
        keys[d * tok:(d + 1) * tok, :] = keys_t[d].T
    far_keys = keys[:2 * tok, :]

    def far_scores(h):
        span = slice(h * tok, (h + 2) * tok)
        scores[:2 * tok, span] = dot(far_keys, q_v[:, span])
        grad_w[:2 * tok, span] = dot(far_keys[:, :value_width], g_t[:, span])

    def softmax(h):
        span = slice(h * tok, (h + 1) * tok)
        far = scores[:2 * tok, span] * scale2 + bias[:2 * tok, :]
        own = scores[2 * tok:, span]
        highest = jnp.maximum(
            jnp.max(far, axis=0, keepdims=True), jnp.max(own, axis=0, keepdims=True)
        )
        exps = [jnp.exp2(far - highest), jnp.exp2(own - highest)]
        grads = [grad_w[:2 * tok, span], grad_w[2 * tok:, span]]
        total = sum(jnp.sum(e, axis=0, keepdims=True) for e in exps)
        inverse = 1.0 / total
        row_dot = inverse * sum(
            jnp.sum(e * g, axis=0, keepdims=True) for e, g in zip(exps, grads)
        )
        for e, g, rows_of in zip(exps, grads, (slice(0, 2 * tok), slice(2 * tok, 3 * tok))):
            weight = e * inverse
            d_scores[rows_of, span] = (weight * (g - row_dot) * scale).astype(BF16)
            weights[rows_of, span] = weight.astype(BF16)

    def partial_sum(first, last, span):
        q_part = dot(q_v[:, span], d_scores[first:last, span], True)
        g_part = dot(g_t[:, span], weights[first:last, span], True)
        return q_part[:value_width] + g_part, q_part[value_width:]

    far_scores(0)
    for h in range(0, heads, 2):
        if h + 2 < heads:
            far_scores(h + 2)
        softmax(h)
        softmax(h + 1)
        top, bottom = partial_sum(0, 2 * tok, slice(h * tok, (h + 2) * tok))
        if h > 0:
            top = top + part_sum[:value_width, :]
            bottom = bottom + part_sum[value_width:, :]
        if h + 2 < heads:
            part_sum[:value_width, :] = top
            part_sum[value_width:, :] = bottom
    for d in range(2):
        part_out[d, :value_width, :] = top[:, d * tok:(d + 1) * tok].astype(BF16)
        part_out[d, value_width:key_width, :] = bottom[:, d * tok:(d + 1) * tok].astype(BF16)

    def piece(i):
        return pl.ds(pl.multiple_of(lax.rem(head + 1 + i, n_head) * rows, 16), rows)

    def send_part(source, target_ref, recv_sem, i, other):
        return pltpu.make_async_remote_copy(
            src_ref=part_out.at[source, piece(i)], dst_ref=target_ref.at[piece(i)],
            send_sem=part_send.at[source, i], recv_sem=recv_sem.at[i],
            device_id=(other, head), device_id_type=MESH,
        )

    far_parts = [send_part(0, part_in.at[0], part_recv.at[0], i, behind[1]) for i in range(n_head)]
    near_parts = [send_part(1, part_in.at[1], part_recv.at[1], i, behind[0]) for i in range(n_head)]
    relayed = [send_part(0, relay_in, relay_recv, i, behind[0]) for i in range(n_head)]

    @pl.when(even)
    def _():
        for copy in far_parts:
            copy.start()
        for i in range(n_head):
            here = piece(i)
            relayed[i].wait_recv()
            joined = part_out[1, here, :].astype(F32) + relay_in[here, :].astype(F32)
            part_out[1, here, :] = joined.astype(BF16)
            near_parts[i].start()

    @pl.when(jnp.logical_not(even))
    def _():
        part_in[0] = jnp.zeros_like(part_in[0])
        for i in range(n_head):
            relayed[i].start()
        for copy in near_parts:
            copy.start()

    top, bottom = partial_sum(2 * tok, 3 * tok, slice(0, cols))
    own_sum[:value_width, :] = top
    own_sum[value_width:key_width, :] = bottom

    def reduce_piece(i):
        near_parts[i].wait_recv()

        @pl.when(even)
        def _():
            far_parts[i].wait_recv()

        here = piece(i)
        return own_sum[here, :] + part_in[0, here, :].astype(F32) + part_in[1, here, :].astype(F32)

    gq_copies = []

    def grad_queries(first, last):
        all_keys = jnp.concatenate([keys_t[0], keys_t[1], keys_t[2]], axis=1)
        span = slice(first * tok, last * tok)
        gq_v[:, span] = dot(all_keys, d_scores[:, span]).astype(BF16)
        for h in range(first, last):
            copy = pltpu.make_async_copy(
                gq_v.at[:, h * tok:(h + 1) * tok], gq_hbm.at[h], gq_sem.at[h]
            )
            copy.start()
            gq_copies.append(copy)

    grad_queries(0, heads)

    head_copies = []
    for i in range(n_head - 1):
        head_out[i] = reduce_piece(i).astype(BF16)
        copy = pltpu.make_async_remote_copy(
            src_ref=head_out.at[i], dst_ref=head_in.at[i],
            send_sem=head_send.at[i], recv_sem=head_recv.at[i],
            device_id=(seq, peers[i]), device_id_type=MESH,
        )
        copy.start()
        head_copies.append(copy)
    total = reduce_piece(n_head - 1)
    for i in range(n_head - 1):
        head_copies[i].wait_recv()
        total = total + head_in[i].astype(F32)
    mine = piece(n_head - 1)
    final[mine, :] = total.astype(BF16)
    final_copies = []
    for i in range(n_head - 1):
        copy = pltpu.make_async_remote_copy(
            src_ref=final.at[mine], dst_ref=final.at[mine],
            send_sem=final_send.at[i], recv_sem=final_recv.at[i],
            device_id=(seq, peers[i]), device_id_type=MESH,
        )
        copy.start()
        final_copies.append(copy)
    for copy in final_copies:
        copy.wait_recv()
    gl_ref[...] = final[:key_width, :]
    for copy in near_keys + near_parts + head_copies + final_copies:
        copy.wait_send()

    @pl.when(even)
    def _():
        for copy in far_sends + passed_on + far_parts:
            copy.wait_send()

    @pl.when(jnp.logical_not(even))
    def _():
        for copy in relayed:
            copy.wait_send()

    for copy in gq_copies:
        copy.wait()


def write_back(gq_ref, gl_ref, gq_out, gl_out, sem):
    heads = gq_ref.shape[0]
    copies = [pltpu.make_async_copy(gl_ref, gl_out, sem.at[heads])]
    for h in range(heads):
        copies.append(pltpu.make_async_copy(gq_ref.at[h], gq_out.at[h], sem.at[h]))
    for copy in copies:
        copy.start()
    for copy in copies:
        copy.wait()


def on_device(n_seq, n_head, queries, latent, grad_out, lookback):
    tok, heads, key_width = queries.shape
    value_width = grad_out.shape[2]
    cols = heads * tok
    rows = -(-key_width // (n_head * 16)) * 16
    padded = rows * n_head
    dma = pltpu.SemaphoreType.DMA
    flops = 2 * 3 * tok * cols * (3 * key_width + 2 * value_width)
    operands = [
        pltpu.with_memory_space_constraint(value, pltpu.HBM)
        for value in (
            queries.transpose(1, 2, 0),
            latent.T,
            grad_out.reshape(tok * heads, value_width),
            lookback.reshape(1, tok),
        )
    ]
    grad_q, grad_l = pl.pallas_call(
        functools.partial(kernel, n_seq, n_head, rows),
        out_shape=(
            jax.ShapeDtypeStruct((heads, key_width, tok), BF16),
            jax.ShapeDtypeStruct((key_width, tok), BF16),
        ),
        in_specs=[pl.BlockSpec(memory_space=pltpu.HBM)] * 4,
        out_specs=(pl.BlockSpec(memory_space=pl.ANY), pl.BlockSpec(memory_space=pltpu.VMEM)),
        scratch_shapes=[
            pltpu.VMEM((1, tok), jnp.int32),
            pltpu.VMEM((key_width, cols), BF16),
            pltpu.VMEM((cols, value_width), BF16),
            pltpu.VMEM((value_width // 128, cols, 128), F32),
            pltpu.VMEM((value_width, cols), BF16),
            pltpu.VMEM((3, key_width, tok), BF16),
            pltpu.VMEM((3 * tok, key_width), BF16),
            pltpu.VMEM((3 * tok, cols), F32),
            pltpu.VMEM((3 * tok, cols), F32),
            pltpu.VMEM((3 * tok, tok), F32),
            pltpu.VMEM((key_width, 2 * tok), F32),
            pltpu.VMEM((3 * tok, cols), BF16),
            pltpu.VMEM((3 * tok, cols), BF16),
            pltpu.VMEM((key_width, cols), BF16),
            pltpu.VMEM((2, padded, tok), BF16),
            pltpu.VMEM((2, padded, tok), BF16),
            pltpu.VMEM((padded, tok), BF16),
            pltpu.VMEM((padded, tok), F32),
            pltpu.VMEM((n_head - 1, rows, tok), BF16),
            pltpu.VMEM((n_head - 1, rows, tok), BF16),
            pltpu.VMEM((padded, tok), BF16),
            dma((3 + heads,)),
            dma((heads,)),
            dma((3, 2, KEY_CHUNKS)),
            dma((2, KEY_CHUNKS)),
            dma((2, n_head)),
            dma((2, n_head)),
            dma((n_head,)),
            dma((n_head - 1,)),
            dma((n_head - 1,)),
            dma((n_head - 1,)),
            dma((n_head - 1,)),
        ],
        compiler_params=pltpu.CompilerParams(
            collective_id=0, has_side_effects=True, vmem_limit_bytes=40 * 1024 * 1024
        ),
        cost_estimate=pl.CostEstimate(
            flops=flops, bytes_accessed=8 * cols * key_width, transcendentals=3 * tok * cols
        ),
        name="latent_backward",
    )(*operands)
    grad_q, grad_l = pl.pallas_call(
        write_back,
        out_shape=(
            jax.ShapeDtypeStruct(grad_q.shape, BF16),
            jax.ShapeDtypeStruct(grad_l.shape, BF16),
        ),
        in_specs=[pl.BlockSpec(memory_space=pl.ANY)] * 2,
        out_specs=(pl.BlockSpec(memory_space=pltpu.HBM),) * 2,
        scratch_shapes=[dma((heads + 1,))],
        compiler_params=pltpu.CompilerParams(vmem_limit_bytes=1024 * 1024),
        name="write_back",
    )(grad_q, grad_l)
    return grad_q.transpose(2, 0, 1), grad_l.T


def solution(mesh):
    return jax.shard_map(
        functools.partial(on_device, mesh.shape["seq"], mesh.shape["head"]),
        mesh=mesh,
        in_specs=(P("seq", "head", None), P("seq", None), P("seq", "head", None), P("seq")),
        out_specs=(P("seq", "head", None), P("seq", None)),
        check_vma=False,
    )
```

```python
import functools

import jax
import jax.numpy as jnp
from jax import lax
from jax.experimental import pallas as pl
from jax.experimental.pallas import tpu as pltpu
from jax.sharding import PartitionSpec as P

ROPE = 64
NOPE = 128
KEY_CHUNKS = 4
LOG2E = 1.4426950408889634
MESH = pl.DeviceIdType.MESH
F32 = jnp.float32
BF16 = jnp.bfloat16


def dot(a, b, trans_b=False):
    dims = (((1,), (1 if trans_b else 0,)), ((), ()))
    return lax.dot_general(a, b, dims, preferred_element_type=F32)


def kernel(
    n_seq, n_head, rows,
    q_hbm, k_hbm, g_hbm, look_hbm, gq_hbm, gl_ref,
    look_ref, q_v, g_v, g_wide, g_t, keys_t, keys, scores, grad_w, bias, part_sum, d_scores, weights, gq_v,
    part_out, part_in, relay_in, own_sum, head_out, head_in, final,
    load_sem, gq_sem, key_send, key_recv, part_send, part_recv, relay_recv,
    head_send, head_recv, final_send, final_recv,
):
    heads, key_width, tok = q_hbm.shape
    value_width = g_hbm.shape[1]
    cols = heads * tok
    scale = (NOPE + ROPE) ** (-0.5)
    scale2 = scale * LOG2E
    seq, head = lax.axis_index("seq"), lax.axis_index("head")
    ahead = [lax.rem(seq + d, n_seq) for d in (1, 2)]
    behind = [lax.rem(seq + n_seq - d, n_seq) for d in (1, 2)]
    peers = [lax.rem(head + 1 + i, n_head) for i in range(n_head - 1)]

    own_copy = pltpu.make_async_copy(k_hbm, keys_t.at[2], load_sem.at[0])
    own_copy.start()
    g_copy = pltpu.make_async_copy(g_hbm, g_v, load_sem.at[1])
    g_copy.start()
    q_copies = [
        pltpu.make_async_copy(q_hbm.at[h], q_v.at[:, h * tok:(h + 1) * tok], load_sem.at[2 + h])
        for h in range(heads)
    ]
    look_copy = pltpu.make_async_copy(look_hbm, look_ref, load_sem.at[2 + heads])
    for copy in q_copies + [look_copy]:
        copy.start()

    barrier = pltpu.get_barrier_semaphore()
    for other in ahead + behind:
        pl.semaphore_signal(barrier, inc=1, device_id=(other, head), device_id_type=MESH)
    for other in peers:
        pl.semaphore_signal(barrier, inc=1, device_id=(seq, other), device_id_type=MESH)
    pl.semaphore_wait(barrier, 4 + n_head - 1)

    own_copy.wait()
    even = lax.rem(seq, 2) == 0
    chunk = key_width // KEY_CHUNKS

    def send_keys(source, target, c, other):
        span = pl.ds(c * chunk, chunk)
        return pltpu.make_async_remote_copy(
            src_ref=keys_t.at[source, span], dst_ref=keys_t.at[target, span],
            send_sem=key_send.at[source, target, c], recv_sem=key_recv.at[target, c],
            device_id=(other, head), device_id_type=MESH,
        )

    near_keys = [send_keys(2, 1, c, ahead[0]) for c in range(KEY_CHUNKS)]
    far_sends = [send_keys(2, 0, c, ahead[1]) for c in range(KEY_CHUNKS)]
    passed_on = [send_keys(1, 0, c, ahead[0]) for c in range(KEY_CHUNKS)]
    for copy in near_keys:
        copy.start()

    @pl.when(even)
    def _():
        for copy in far_sends:
            copy.start()

    keys[2 * tok:, :] = keys_t[2].T
    g_copy.wait()
    for c in range(value_width // 128):
        part = slice(c * 128, (c + 1) * 128)
        g_wide[c] = g_v[:, part].astype(F32)
        for h in range(heads):
            block = g_wide[c, pl.ds(h, tok, stride=heads), :].astype(BF16)
            g_t[part, h * tok:(h + 1) * tok] = block.T
    for copy in q_copies:
        copy.wait()
    look_copy.wait()
    key_pos = lax.broadcasted_iota(jnp.int32, (3 * tok, tok), 0)
    query_pos = lax.broadcasted_iota(jnp.int32, (3 * tok, tok), 1) + 2 * tok
    allowed = (
        (key_pos <= query_pos)
        & (key_pos >= query_pos - look_ref[...])
        & (key_pos >= (2 - seq) * tok)
    )
    bias[...] = jnp.where(allowed, 0.0, -jnp.inf)
    own_keys = keys[2 * tok:, :]
    for h in range(0, heads, 2):
        span = slice(h * tok, (h + 2) * tok)
        own_bias = bias[2 * tok:, :]
        scores[2 * tok:, span] = dot(own_keys, q_v[:, span]) * scale2 + jnp.concatenate(
            [own_bias, own_bias], axis=1
        )
        grad_w[2 * tok:, span] = dot(own_keys[:, :value_width], g_t[:, span])

    @pl.when(even)
    def _():
        for c in range(KEY_CHUNKS):
            near_keys[c].wait_recv()
            passed_on[c].start()

    @pl.when(jnp.logical_not(even))
    def _():
        for copy in near_keys:
            copy.wait_recv()

    for copy in far_sends:
        copy.wait_recv()
    for d in range(2):
        keys[d * tok:(d + 1) * tok, :] = keys_t[d].T
    far_keys = keys[:2 * tok, :]

    def far_scores(h):
        span = slice(h * tok, (h + 2) * tok)
        scores[:2 * tok, span] = dot(far_keys, q_v[:, span])
        grad_w[:2 * tok, span] = dot(far_keys[:, :value_width], g_t[:, span])

    def softmax(h):
        span = slice(h * tok, (h + 1) * tok)
        far = scores[:2 * tok, span] * scale2 + bias[:2 * tok, :]
        own = scores[2 * tok:, span]
        highest = jnp.maximum(
            jnp.max(far, axis=0, keepdims=True), jnp.max(own, axis=0, keepdims=True)
        )
        exps = [jnp.exp2(far - highest), jnp.exp2(own - highest)]
        grads = [grad_w[:2 * tok, span], grad_w[2 * tok:, span]]
        total = sum(jnp.sum(e, axis=0, keepdims=True) for e in exps)
        inverse = 1.0 / total
        row_dot = inverse * sum(
            jnp.sum(e * g, axis=0, keepdims=True) for e, g in zip(exps, grads)
        )
        for e, g, rows_of in zip(exps, grads, (slice(0, 2 * tok), slice(2 * tok, 3 * tok))):
            weight = e * inverse
            d_scores[rows_of, span] = (weight * (g - row_dot) * scale).astype(BF16)
            weights[rows_of, span] = weight.astype(BF16)

    def partial_sum(first, last, span):
        q_part = dot(q_v[:, span], d_scores[first:last, span], True)
        g_part = dot(g_t[:, span], weights[first:last, span], True)
        return q_part[:value_width] + g_part, q_part[value_width:]

    far_scores(0)
    for h in range(0, heads, 2):
        if h + 2 < heads:
            far_scores(h + 2)
        softmax(h)
        softmax(h + 1)
        top, bottom = partial_sum(0, 2 * tok, slice(h * tok, (h + 2) * tok))
        if h > 0:
            top = top + part_sum[:value_width, :]
            bottom = bottom + part_sum[value_width:, :]
        if h + 2 < heads:
            part_sum[:value_width, :] = top
            part_sum[value_width:, :] = bottom
    for d in range(2):
        part_out[d, :value_width, :] = top[:, d * tok:(d + 1) * tok].astype(BF16)
        part_out[d, value_width:key_width, :] = bottom[:, d * tok:(d + 1) * tok].astype(BF16)

    def piece(i):
        return pl.ds(pl.multiple_of(lax.rem(head + 1 + i, n_head) * rows, 16), rows)

    def send_part(source, target_ref, recv_sem, i, other):
        return pltpu.make_async_remote_copy(
            src_ref=part_out.at[source, piece(i)], dst_ref=target_ref.at[piece(i)],
            send_sem=part_send.at[source, i], recv_sem=recv_sem.at[i],
            device_id=(other, head), device_id_type=MESH,
        )

    far_parts = [send_part(0, part_in.at[0], part_recv.at[0], i, behind[1]) for i in range(n_head)]
    near_parts = [send_part(1, part_in.at[1], part_recv.at[1], i, behind[0]) for i in range(n_head)]
    relayed = [send_part(0, relay_in, relay_recv, i, behind[0]) for i in range(n_head)]

    @pl.when(even)
    def _():
        for copy in far_parts:
            copy.start()

    @pl.when(jnp.logical_not(even))
    def _():
        part_in[0] = jnp.zeros_like(part_in[0])
        for i in range(n_head):
            relayed[i].start()
        for copy in near_parts:
            copy.start()

    top, bottom = partial_sum(2 * tok, 3 * tok, slice(0, cols))
    own_sum[:value_width, :] = top
    own_sum[value_width:key_width, :] = bottom

    @pl.when(even)
    def _():
        for i in range(n_head):
            here = piece(i)
            relayed[i].wait_recv()
            joined = part_out[1, here, :].astype(F32) + relay_in[here, :].astype(F32)
            part_out[1, here, :] = joined.astype(BF16)
            near_parts[i].start()

    def reduce_piece(i):
        near_parts[i].wait_recv()

        @pl.when(even)
        def _():
            far_parts[i].wait_recv()

        here = piece(i)
        return own_sum[here, :] + part_in[0, here, :].astype(F32) + part_in[1, here, :].astype(F32)

    gq_copies = []

    def grad_queries(first, last):
        all_keys = jnp.concatenate([keys_t[0], keys_t[1], keys_t[2]], axis=1)
        span = slice(first * tok, last * tok)
        gq_v[:, span] = dot(all_keys, d_scores[:, span]).astype(BF16)
        for h in range(first, last):
            copy = pltpu.make_async_copy(
                gq_v.at[:, h * tok:(h + 1) * tok], gq_hbm.at[h], gq_sem.at[h]
            )
            copy.start()
            gq_copies.append(copy)

    head_copies = []
    for i in range(n_head - 1):
        head_out[i] = reduce_piece(i).astype(BF16)
        copy = pltpu.make_async_remote_copy(
            src_ref=head_out.at[i], dst_ref=head_in.at[i],
            send_sem=head_send.at[i], recv_sem=head_recv.at[i],
            device_id=(seq, peers[i]), device_id_type=MESH,
        )
        copy.start()
        head_copies.append(copy)
    grad_queries(0, heads)

    total = reduce_piece(n_head - 1)
    for i in range(n_head - 1):
        head_copies[i].wait_recv()
        total = total + head_in[i].astype(F32)
    mine = piece(n_head - 1)
    final[mine, :] = total.astype(BF16)
    final_copies = []
    for i in range(n_head - 1):
        copy = pltpu.make_async_remote_copy(
            src_ref=final.at[mine], dst_ref=final.at[mine],
            send_sem=final_send.at[i], recv_sem=final_recv.at[i],
            device_id=(seq, peers[i]), device_id_type=MESH,
        )
        copy.start()
        final_copies.append(copy)
    for copy in final_copies:
        copy.wait_recv()
    gl_ref[...] = final[:key_width, :]
    for copy in near_keys + near_parts + head_copies + final_copies:
        copy.wait_send()

    @pl.when(even)
    def _():
        for copy in far_sends + passed_on + far_parts:
            copy.wait_send()

    @pl.when(jnp.logical_not(even))
    def _():
        for copy in relayed:
            copy.wait_send()

    for copy in gq_copies:
        copy.wait()


def write_back(gq_ref, gl_ref, gq_out, gl_out, sem):
    heads = gq_ref.shape[0]
    copies = [pltpu.make_async_copy(gl_ref, gl_out, sem.at[heads])]
    for h in range(heads):
        copies.append(pltpu.make_async_copy(gq_ref.at[h], gq_out.at[h], sem.at[h]))
    for copy in copies:
        copy.start()
    for copy in copies:
        copy.wait()


def on_device(n_seq, n_head, queries, latent, grad_out, lookback):
    tok, heads, key_width = queries.shape
    value_width = grad_out.shape[2]
    cols = heads * tok
    rows = -(-key_width // (n_head * 16)) * 16
    padded = rows * n_head
    dma = pltpu.SemaphoreType.DMA
    flops = 2 * 3 * tok * cols * (3 * key_width + 2 * value_width)
    operands = [
        pltpu.with_memory_space_constraint(value, pltpu.HBM)
        for value in (
            queries.transpose(1, 2, 0),
            latent.T,
            grad_out.reshape(tok * heads, value_width),
            lookback.reshape(1, tok),
        )
    ]
    grad_q, grad_l = pl.pallas_call(
        functools.partial(kernel, n_seq, n_head, rows),
        out_shape=(
            jax.ShapeDtypeStruct((heads, key_width, tok), BF16),
            jax.ShapeDtypeStruct((key_width, tok), BF16),
        ),
        in_specs=[pl.BlockSpec(memory_space=pltpu.HBM)] * 4,
        out_specs=(pl.BlockSpec(memory_space=pl.ANY), pl.BlockSpec(memory_space=pltpu.VMEM)),
        scratch_shapes=[
            pltpu.VMEM((1, tok), jnp.int32),
            pltpu.VMEM((key_width, cols), BF16),
            pltpu.VMEM((cols, value_width), BF16),
            pltpu.VMEM((value_width // 128, cols, 128), F32),
            pltpu.VMEM((value_width, cols), BF16),
            pltpu.VMEM((3, key_width, tok), BF16),
            pltpu.VMEM((3 * tok, key_width), BF16),
            pltpu.VMEM((3 * tok, cols), F32),
            pltpu.VMEM((3 * tok, cols), F32),
            pltpu.VMEM((3 * tok, tok), F32),
            pltpu.VMEM((key_width, 2 * tok), F32),
            pltpu.VMEM((3 * tok, cols), BF16),
            pltpu.VMEM((3 * tok, cols), BF16),
            pltpu.VMEM((key_width, cols), BF16),
            pltpu.VMEM((2, padded, tok), BF16),
            pltpu.VMEM((2, padded, tok), BF16),
            pltpu.VMEM((padded, tok), BF16),
            pltpu.VMEM((padded, tok), F32),
            pltpu.VMEM((n_head - 1, rows, tok), BF16),
            pltpu.VMEM((n_head - 1, rows, tok), BF16),
            pltpu.VMEM((padded, tok), BF16),
            dma((3 + heads,)),
            dma((heads,)),
            dma((3, 2, KEY_CHUNKS)),
            dma((2, KEY_CHUNKS)),
            dma((2, n_head)),
            dma((2, n_head)),
            dma((n_head,)),
            dma((n_head - 1,)),
            dma((n_head - 1,)),
            dma((n_head - 1,)),
            dma((n_head - 1,)),
        ],
        compiler_params=pltpu.CompilerParams(
            collective_id=0, has_side_effects=True, vmem_limit_bytes=40 * 1024 * 1024
        ),
        cost_estimate=pl.CostEstimate(
            flops=flops, bytes_accessed=8 * cols * key_width, transcendentals=3 * tok * cols
        ),
        name="latent_backward",
    )(*operands)
    grad_q, grad_l = pl.pallas_call(
        write_back,
        out_shape=(
            jax.ShapeDtypeStruct(grad_q.shape, BF16),
            jax.ShapeDtypeStruct(grad_l.shape, BF16),
        ),
        in_specs=[pl.BlockSpec(memory_space=pl.ANY)] * 2,
        out_specs=(pl.BlockSpec(memory_space=pltpu.HBM),) * 2,
        scratch_shapes=[dma((heads + 1,))],
        compiler_params=pltpu.CompilerParams(vmem_limit_bytes=1024 * 1024),
        name="write_back",
    )(grad_q, grad_l)
    return grad_q.transpose(2, 0, 1), grad_l.T


def solution(mesh):
    return jax.shard_map(
        functools.partial(on_device, mesh.shape["seq"], mesh.shape["head"]),
        mesh=mesh,
        in_specs=(P("seq", "head", None), P("seq", None), P("seq", "head", None), P("seq")),
        out_specs=(P("seq", "head", None), P("seq", None)),
        check_vma=False,
    )
```

```python
import functools

import jax
import jax.numpy as jnp
from jax import lax
from jax.experimental import pallas as pl
from jax.experimental.pallas import tpu as pltpu
from jax.sharding import PartitionSpec as P

ROPE = 64
NOPE = 128
KEY_CHUNKS = 4
LOG2E = 1.4426950408889634
MESH = pl.DeviceIdType.MESH
F32 = jnp.float32
BF16 = jnp.bfloat16


def dot(a, b, trans_b=False):
    dims = (((1,), (1 if trans_b else 0,)), ((), ()))
    return lax.dot_general(a, b, dims, preferred_element_type=F32)


def kernel(
    n_seq, n_head, rows,
    q_hbm, k_hbm, g_hbm, look_hbm, gq_hbm, gl_ref,
    look_ref, q_v, g_v, g_wide, g_t, keys_t, keys, scores, grad_w, bias, part_sum, d_scores, weights, gq_v,
    part_out, part_in, relay_in, own_sum, head_out, head_in, final,
    load_sem, gq_sem, key_send, key_recv, part_send, part_recv, relay_recv,
    head_send, head_recv, final_send, final_recv,
):
    heads, key_width, tok = q_hbm.shape
    value_width = g_hbm.shape[1]
    cols = heads * tok
    scale = (NOPE + ROPE) ** (-0.5)
    scale2 = scale * LOG2E
    seq, head = lax.axis_index("seq"), lax.axis_index("head")
    ahead = [lax.rem(seq + d, n_seq) for d in (1, 2)]
    behind = [lax.rem(seq + n_seq - d, n_seq) for d in (1, 2)]
    peers = [lax.rem(head + 1 + i, n_head) for i in range(n_head - 1)]

    own_copy = pltpu.make_async_copy(k_hbm, keys_t.at[2], load_sem.at[0])
    own_copy.start()
    g_copy = pltpu.make_async_copy(g_hbm, g_v, load_sem.at[1])
    g_copy.start()
    q_copies = [
        pltpu.make_async_copy(q_hbm.at[h], q_v.at[:, h * tok:(h + 1) * tok], load_sem.at[2 + h])
        for h in range(heads)
    ]
    look_copy = pltpu.make_async_copy(look_hbm, look_ref, load_sem.at[2 + heads])
    for copy in q_copies + [look_copy]:
        copy.start()

    barrier = pltpu.get_barrier_semaphore()
    even = lax.rem(seq, 2) == 0

    def greet(other_seq, other_head):
        pl.semaphore_signal(
            barrier, inc=1, device_id=(other_seq, other_head), device_id_type=MESH
        )

    for other in (ahead[0], behind[0]):
        greet(other, head)
    for other in peers:
        greet(seq, other)

    @pl.when(even)
    def _():
        for other in (ahead[1], behind[1]):
            greet(other, head)
        pl.semaphore_wait(barrier, 4 + n_head - 1)

    @pl.when(jnp.logical_not(even))
    def _():
        pl.semaphore_wait(barrier, 2 + n_head - 1)

    own_copy.wait()
    chunk = key_width // KEY_CHUNKS

    def send_keys(source, target, c, other):
        span = pl.ds(c * chunk, chunk)
        return pltpu.make_async_remote_copy(
            src_ref=keys_t.at[source, span], dst_ref=keys_t.at[target, span],
            send_sem=key_send.at[source, target, c], recv_sem=key_recv.at[target, c],
            device_id=(other, head), device_id_type=MESH,
        )

    near_keys = [send_keys(2, 1, c, ahead[0]) for c in range(KEY_CHUNKS)]
    far_sends = [send_keys(2, 0, c, ahead[1]) for c in range(KEY_CHUNKS)]
    passed_on = [send_keys(1, 0, c, ahead[0]) for c in range(KEY_CHUNKS)]
    for copy in near_keys:
        copy.start()

    @pl.when(even)
    def _():
        for copy in far_sends:
            copy.start()

    keys[2 * tok:, :] = keys_t[2].T
    g_copy.wait()
    for c in range(value_width // 128):
        part = slice(c * 128, (c + 1) * 128)
        g_wide[c] = g_v[:, part].astype(F32)
        for h in range(heads):
            block = g_wide[c, pl.ds(h, tok, stride=heads), :].astype(BF16)
            g_t[part, h * tok:(h + 1) * tok] = block.T
    for copy in q_copies:
        copy.wait()
    look_copy.wait()
    key_pos = lax.broadcasted_iota(jnp.int32, (3 * tok, tok), 0)
    query_pos = lax.broadcasted_iota(jnp.int32, (3 * tok, tok), 1) + 2 * tok
    allowed = (
        (key_pos <= query_pos)
        & (key_pos >= query_pos - look_ref[...])
        & (key_pos >= (2 - seq) * tok)
    )
    bias[...] = jnp.where(allowed, 0.0, -jnp.inf)
    own_keys = keys[2 * tok:, :]
    for h in range(0, heads, 2):
        span = slice(h * tok, (h + 2) * tok)
        own_bias = bias[2 * tok:, :]
        scores[2 * tok:, span] = dot(own_keys, q_v[:, span]) * scale2 + jnp.concatenate(
            [own_bias, own_bias], axis=1
        )
        grad_w[2 * tok:, span] = dot(own_keys[:, :value_width], g_t[:, span])

    @pl.when(even)
    def _():
        for c in range(KEY_CHUNKS):
            near_keys[c].wait_recv()
            passed_on[c].start()

    @pl.when(jnp.logical_not(even))
    def _():
        for copy in near_keys:
            copy.wait_recv()

    for copy in far_sends:
        copy.wait_recv()
    for d in range(2):
        keys[d * tok:(d + 1) * tok, :] = keys_t[d].T
    far_keys = keys[:2 * tok, :]

    def far_scores(h):
        span = slice(h * tok, (h + 2) * tok)
        scores[:2 * tok, span] = dot(far_keys, q_v[:, span])
        grad_w[:2 * tok, span] = dot(far_keys[:, :value_width], g_t[:, span])

    def softmax(h):
        span = slice(h * tok, (h + 1) * tok)
        far = scores[:2 * tok, span] * scale2 + bias[:2 * tok, :]
        own = scores[2 * tok:, span]
        highest = jnp.maximum(
            jnp.max(far, axis=0, keepdims=True), jnp.max(own, axis=0, keepdims=True)
        )
        exps = [jnp.exp2(far - highest), jnp.exp2(own - highest)]
        grads = [grad_w[:2 * tok, span], grad_w[2 * tok:, span]]
        total = sum(jnp.sum(e, axis=0, keepdims=True) for e in exps)
        inverse = 1.0 / total
        row_dot = inverse * sum(
            jnp.sum(e * g, axis=0, keepdims=True) for e, g in zip(exps, grads)
        )
        for e, g, rows_of in zip(exps, grads, (slice(0, 2 * tok), slice(2 * tok, 3 * tok))):
            weight = e * inverse
            d_scores[rows_of, span] = (weight * (g - row_dot) * scale).astype(BF16)
            weights[rows_of, span] = weight.astype(BF16)

    def partial_sum(first, last, span):
        q_part = dot(q_v[:, span], d_scores[first:last, span], True)
        g_part = dot(g_t[:, span], weights[first:last, span], True)
        return q_part[:value_width] + g_part, q_part[value_width:]

    far_scores(0)
    for h in range(0, heads, 2):
        if h + 2 < heads:
            far_scores(h + 2)
        softmax(h)
        softmax(h + 1)
        top, bottom = partial_sum(0, 2 * tok, slice(h * tok, (h + 2) * tok))
        if h > 0:
            top = top + part_sum[:value_width, :]
            bottom = bottom + part_sum[value_width:, :]
        if h + 2 < heads:
            part_sum[:value_width, :] = top
            part_sum[value_width:, :] = bottom
    for d in range(2):
        part_out[d, :value_width, :] = top[:, d * tok:(d + 1) * tok].astype(BF16)
        part_out[d, value_width:key_width, :] = bottom[:, d * tok:(d + 1) * tok].astype(BF16)

    def piece(i):
        return pl.ds(pl.multiple_of(lax.rem(head + 1 + i, n_head) * rows, 16), rows)

    def send_part(source, target_ref, recv_sem, i, other):
        return pltpu.make_async_remote_copy(
            src_ref=part_out.at[source, piece(i)], dst_ref=target_ref.at[piece(i)],
            send_sem=part_send.at[source, i], recv_sem=recv_sem.at[i],
            device_id=(other, head), device_id_type=MESH,
        )

    far_parts = [send_part(0, part_in.at[0], part_recv.at[0], i, behind[1]) for i in range(n_head)]
    near_parts = [send_part(1, part_in.at[1], part_recv.at[1], i, behind[0]) for i in range(n_head)]
    relayed = [send_part(0, relay_in, relay_recv, i, behind[0]) for i in range(n_head)]

    @pl.when(even)
    def _():
        for copy in far_parts:
            copy.start()

    @pl.when(jnp.logical_not(even))
    def _():
        part_in[0] = jnp.zeros_like(part_in[0])
        for i in range(n_head):
            relayed[i].start()
        for copy in near_parts:
            copy.start()

    top, bottom = partial_sum(2 * tok, 3 * tok, slice(0, cols))
    own_sum[:value_width, :] = top
    own_sum[value_width:key_width, :] = bottom

    @pl.when(even)
    def _():
        for i in range(n_head):
            here = piece(i)
            relayed[i].wait_recv()
            joined = part_out[1, here, :].astype(F32) + relay_in[here, :].astype(F32)
            part_out[1, here, :] = joined.astype(BF16)
            near_parts[i].start()

    def reduce_piece(i):
        near_parts[i].wait_recv()

        @pl.when(even)
        def _():
            far_parts[i].wait_recv()

        here = piece(i)
        return own_sum[here, :] + part_in[0, here, :].astype(F32) + part_in[1, here, :].astype(F32)

    gq_copies = []

    def grad_queries(first, last):
        all_keys = jnp.concatenate([keys_t[0], keys_t[1], keys_t[2]], axis=1)
        span = slice(first * tok, last * tok)
        gq_v[:, span] = dot(all_keys, d_scores[:, span]).astype(BF16)
        for h in range(first, last):
            copy = pltpu.make_async_copy(
                gq_v.at[:, h * tok:(h + 1) * tok], gq_hbm.at[h], gq_sem.at[h]
            )
            copy.start()
            gq_copies.append(copy)

    head_copies = []
    for i in range(n_head - 1):
        head_out[i] = reduce_piece(i).astype(BF16)
        copy = pltpu.make_async_remote_copy(
            src_ref=head_out.at[i], dst_ref=head_in.at[i],
            send_sem=head_send.at[i], recv_sem=head_recv.at[i],
            device_id=(seq, peers[i]), device_id_type=MESH,
        )
        copy.start()
        head_copies.append(copy)
    grad_queries(0, heads)

    total = reduce_piece(n_head - 1)
    for i in range(n_head - 1):
        head_copies[i].wait_recv()
        total = total + head_in[i].astype(F32)
    mine = piece(n_head - 1)
    final[mine, :] = total.astype(BF16)
    final_copies = []
    for i in range(n_head - 1):
        copy = pltpu.make_async_remote_copy(
            src_ref=final.at[mine], dst_ref=final.at[mine],
            send_sem=final_send.at[i], recv_sem=final_recv.at[i],
            device_id=(seq, peers[i]), device_id_type=MESH,
        )
        copy.start()
        final_copies.append(copy)
    for copy in final_copies:
        copy.wait_recv()
    gl_ref[...] = final[:key_width, :]
    for copy in near_keys + near_parts + head_copies + final_copies:
        copy.wait_send()

    @pl.when(even)
    def _():
        for copy in far_sends + passed_on + far_parts:
            copy.wait_send()

    @pl.when(jnp.logical_not(even))
    def _():
        for copy in relayed:
            copy.wait_send()

    for copy in gq_copies:
        copy.wait()


def write_back(gq_ref, gl_ref, gq_out, gl_out, sem):
    heads = gq_ref.shape[0]
    copies = [pltpu.make_async_copy(gl_ref, gl_out, sem.at[heads])]
    for h in range(heads):
        copies.append(pltpu.make_async_copy(gq_ref.at[h], gq_out.at[h], sem.at[h]))
    for copy in copies:
        copy.start()
    for copy in copies:
        copy.wait()


def on_device(n_seq, n_head, queries, latent, grad_out, lookback):
    tok, heads, key_width = queries.shape
    value_width = grad_out.shape[2]
    cols = heads * tok
    rows = -(-key_width // (n_head * 16)) * 16
    padded = rows * n_head
    dma = pltpu.SemaphoreType.DMA
    flops = 2 * 3 * tok * cols * (3 * key_width + 2 * value_width)
    operands = [
        pltpu.with_memory_space_constraint(value, pltpu.HBM)
        for value in (
            queries.transpose(1, 2, 0),
            latent.T,
            grad_out.reshape(tok * heads, value_width),
            lookback.reshape(1, tok),
        )
    ]
    grad_q, grad_l = pl.pallas_call(
        functools.partial(kernel, n_seq, n_head, rows),
        out_shape=(
            jax.ShapeDtypeStruct((heads, key_width, tok), BF16),
            jax.ShapeDtypeStruct((key_width, tok), BF16),
        ),
        in_specs=[pl.BlockSpec(memory_space=pltpu.HBM)] * 4,
        out_specs=(pl.BlockSpec(memory_space=pl.ANY), pl.BlockSpec(memory_space=pltpu.VMEM)),
        scratch_shapes=[
            pltpu.VMEM((1, tok), jnp.int32),
            pltpu.VMEM((key_width, cols), BF16),
            pltpu.VMEM((cols, value_width), BF16),
            pltpu.VMEM((value_width // 128, cols, 128), F32),
            pltpu.VMEM((value_width, cols), BF16),
            pltpu.VMEM((3, key_width, tok), BF16),
            pltpu.VMEM((3 * tok, key_width), BF16),
            pltpu.VMEM((3 * tok, cols), F32),
            pltpu.VMEM((3 * tok, cols), F32),
            pltpu.VMEM((3 * tok, tok), F32),
            pltpu.VMEM((key_width, 2 * tok), F32),
            pltpu.VMEM((3 * tok, cols), BF16),
            pltpu.VMEM((3 * tok, cols), BF16),
            pltpu.VMEM((key_width, cols), BF16),
            pltpu.VMEM((2, padded, tok), BF16),
            pltpu.VMEM((2, padded, tok), BF16),
            pltpu.VMEM((padded, tok), BF16),
            pltpu.VMEM((padded, tok), F32),
            pltpu.VMEM((n_head - 1, rows, tok), BF16),
            pltpu.VMEM((n_head - 1, rows, tok), BF16),
            pltpu.VMEM((padded, tok), BF16),
            dma((3 + heads,)),
            dma((heads,)),
            dma((3, 2, KEY_CHUNKS)),
            dma((2, KEY_CHUNKS)),
            dma((2, n_head)),
            dma((2, n_head)),
            dma((n_head,)),
            dma((n_head - 1,)),
            dma((n_head - 1,)),
            dma((n_head - 1,)),
            dma((n_head - 1,)),
        ],
        compiler_params=pltpu.CompilerParams(
            collective_id=0, has_side_effects=True, vmem_limit_bytes=40 * 1024 * 1024
        ),
        cost_estimate=pl.CostEstimate(
            flops=flops, bytes_accessed=8 * cols * key_width, transcendentals=3 * tok * cols
        ),
        name="latent_backward",
    )(*operands)
    grad_q, grad_l = pl.pallas_call(
        write_back,
        out_shape=(
            jax.ShapeDtypeStruct(grad_q.shape, BF16),
            jax.ShapeDtypeStruct(grad_l.shape, BF16),
        ),
        in_specs=[pl.BlockSpec(memory_space=pl.ANY)] * 2,
        out_specs=(pl.BlockSpec(memory_space=pltpu.HBM),) * 2,
        scratch_shapes=[dma((heads + 1,))],
        compiler_params=pltpu.CompilerParams(vmem_limit_bytes=1024 * 1024),
        name="write_back",
    )(grad_q, grad_l)
    return grad_q.transpose(2, 0, 1), grad_l.T


def solution(mesh):
    return jax.shard_map(
        functools.partial(on_device, mesh.shape["seq"], mesh.shape["head"]),
        mesh=mesh,
        in_specs=(P("seq", "head", None), P("seq", None), P("seq", "head", None), P("seq")),
        out_specs=(P("seq", "head", None), P("seq", None)),
        check_vma=False,
    )
```
